32 devices in a mesh: feat: 2 (over y), row: 16 (over z, x, core).
Axes of the slice: x: 2, y: 2, z: 4, core: 2. Of those that a mesh axis runs over, the one named last changes fastest.
Arguments:
- bin_values: int32 [32768, 256], P('row', 'feat'), may hold values from 0 to 127
- leaf_ids: int32 [32768], P('row'), may hold values from 0 to 3
- treated: int32 [32768], P('row'), may hold values 0 or 1
- gradient: bfloat16 [32768], P('row'), may hold values from -6 to 6
- hessian: bfloat16 [32768], P('row'), may hold values from 0.099609375 to 2
Outputs:
- split_gain: float32 [4, 256, 128], P(None, ('feat', 'row'))
- best_gain: float32 [4], replicated
The draws below stay inside these ranges and needn't reach their ends.
All inputs are finite; a program needn't handle non-finite values. No bound on the sum of `treated` on one device may be relied on, other than what follows from the above.
Results may differ from the reference program's by a relative error of at most 0.0003.
Values sent between devices are 32-bit elements; how exact they have to be, the bound alone decides.
No kernel may reach another device: no remote copies, remote signals or barrier semaphores. Data moves between devices by JAX's collectives and lax.ppermute only.
A program may use at most 64 MiB of HBM per device.

```python
import math
import jax
import jax.numpy as jnp
import numpy as np
from jax import lax

BINS = 128
LEAVES = 4
F = 256
ROWS = 32768


def plant(result, rng, smallest, largest):
    longest = result.shape.index(max(result.shape))
    spots = []
    for shift in (0, 1):
        where = [jax.random.randint(jax.random.fold_in(rng, axis), (), 0, length) for axis, length in enumerate(result.shape)]
        where[longest] = (where[longest] + shift) % result.shape[longest]
        spots.append(tuple(where))
    return result.at[spots[0]].set(smallest).at[spots[1]].set(largest)


def level_of(rng, shape, pieces, smallest, largest):
    level, own = 1.0, jax.random.fold_in(rng, 6)
    for position, shards_of in pieces:
        steps = jnp.exp(jax.random.uniform(jax.random.fold_in(own, position), (shards_of,), jnp.float32, smallest / len(pieces), largest / len(pieces)))
        level = level * jnp.repeat(steps, shape[position] // shards_of).reshape([-1 if axis == position else 1 for axis in range(len(shape))])
    return level


def rank_bounds(number_of, slope):
    weights = [(1 << 20) // math.isqrt(rank ** slope) + 1 for rank in range(1, number_of + 1)]
    scale = 1 + sum(weights) // (1 << 30)
    return np.cumsum(np.array([max(1, weight // scale) for weight in weights]))


def skewed_ids(rng, shape, count, slope):
    table = rank_bounds(count, slope)
    ticket = jax.random.randint(jax.random.fold_in(rng, 1), shape, 0, int(table[count - 1]))
    rank = jnp.searchsorted(jnp.asarray(table, jnp.int32), ticket, side="right")
    return jax.random.permutation(jax.random.fold_in(rng, 2), count)[rank].astype(jnp.int32)


def scatter_about(rng, shape, deviation, most, pieces=(), held_as=jnp.bfloat16):
    array = deviation * jax.random.normal(rng, shape, jnp.float32)
    if pieces:
        array = array * level_of(rng, shape, pieces, -0.22, 0.18)
    return jnp.clip(array, -most, most).astype(held_as)


def setup_inputs(seed: int = 0) -> dict:
    arg_keys = jax.random.split(jax.random.key(seed), 6)
    return {
        "bin_values": plant(jax.random.randint(arg_keys[0], (ROWS, F), 0, BINS), jax.random.fold_in(arg_keys[0], 1), 0, BINS - 1).astype(jnp.int32),
        "leaf_ids": plant(skewed_ids(arg_keys[1], (ROWS,), LEAVES, 2), jax.random.fold_in(arg_keys[1], 3), 0, LEAVES - 1).astype(jnp.int32),
        "treated": plant((jax.random.randint(arg_keys[2], (ROWS,), 0, 2) < 1).astype(jnp.int32), jax.random.fold_in(arg_keys[2], 1), 0, 1),
        "gradient": scatter_about(arg_keys[3], (ROWS,), 1.0, 6.0, ((0, 16),)),
        "hessian": jnp.clip(jnp.exp(math.log(2.0) - 2.9996462 * jax.random.uniform(arg_keys[4], (ROWS,), jnp.float32) ** level_of(arg_keys[4], (ROWS,), ((0, 16),), -0.2, 0.2)), 0.099609375, 2.0).astype(jnp.bfloat16),
    }


def node_score(totals):
    grad_t = totals[0]
    hess_t = totals[1]
    grad_c = totals[2]
    hess_c = totals[3]
    value_t = grad_t / (hess_t + 1.0)
    value_c = grad_c / (hess_c + 1.0)
    spread = value_t - value_c
    return grad_t * value_t + grad_c * value_c + (hess_t + hess_c) * spread * spread


def reference(bin_values, leaf_ids, treated, gradient, hessian):
    chosen = treated.astype(jnp.float32)
    others = 1.0 - chosen
    grad_full = gradient.astype(jnp.float32)
    hess_full = hessian.astype(jnp.float32)
    columns = jnp.stack([grad_full * chosen, hess_full * chosen, grad_full * others, hess_full * others], axis=1)
    block_width = math.gcd(F, 64)
    blocks = jnp.moveaxis(bin_values.reshape(ROWS, F // block_width, block_width), 1, 0)
    offsets = jnp.arange(block_width, dtype=jnp.int32)[None, :] * (LEAVES * BINS) + leaf_ids[:, None] * BINS
    payload = jnp.broadcast_to(columns[:, None, :], (ROWS, block_width, 4)).reshape(ROWS * block_width, 4)

    def block_hist(feat_block):
        segment_ids = (offsets + feat_block).reshape(-1).astype(jnp.int32)
        return jax.ops.segment_sum(payload, segment_ids, num_segments=block_width * LEAVES * BINS)

    histogram = lax.map(block_hist, blocks).reshape(F, LEAVES, BINS, 4)
    histogram = jnp.transpose(histogram, (3, 1, 0, 2))
    bin_range = jnp.arange(BINS, dtype=jnp.int32)
    ladder = (bin_range[:, None] <= bin_range[None, :]).astype(jnp.float32)
    left_sums = jnp.einsum("slfb,bk->slfk", histogram, ladder, precision=lax.Precision.HIGHEST)
    parent_sums = left_sums[:, :, :, BINS - 1:]
    right_sums = parent_sums - left_sums
    split_gain = node_score(left_sums) + node_score(right_sums) - node_score(parent_sums)
    best_gain = jnp.max(split_gain, axis=(1, 2))
    return split_gain, best_gain
```

```python
import functools

import jax
import jax.numpy as jnp
from jax import lax
from jax.experimental import pallas as pl
from jax.experimental.pallas import tpu as pltpu
from jax.sharding import PartitionSpec as P

BINS = 128
LEAVES = 4
HALF = BINS // 2
STATS = 4 * LEAVES
PACK = 16
NT = (((1,), (1,)), ((), ()))
DEPTH = 256


def reversed_bits(value, bits):
    out = 0
    for i in range(bits):
        out = out + (((value >> i) & 1) << (bits - 1 - i))
    return out


def slot_of(position, kind, bits):
    if kind == "core":
        return reversed_bits(position, bits - 1) * 2 + 1
    if kind == "far":
        return (reversed_bits(position, bits - 2) * 2 + 1) * 2
    return reversed_bits(position, bits - 2) * 4


def stats_of(leaf, treated, gradient, hessian, stats_ref):
    row = lax.broadcasted_iota(jnp.int32, (STATS, 128), 0)
    stat, own_leaf = row // LEAVES, row % LEAVES
    grad, hess = gradient.astype(jnp.float32), hessian.astype(jnp.float32)
    for i in range(leaf.shape[0]):
        wide = lambda x: jnp.broadcast_to(x[i : i + 1], (STATS, 128))
        value = jnp.where(stat % 2 == 0, wide(grad), wide(hess))
        ok = (wide(leaf) == own_leaf) & ((wide(treated) == 1) == (stat < 2))
        stats_ref[:, i * 128 : (i + 1) * 128] = jnp.where(ok, value, 0.0).astype(jnp.bfloat16)


def left_sums_of(me, kind, bits, share, high_ref, low_ref, stats_ref, out_ref):
    rows = high_ref.shape[1]
    steps = lax.broadcasted_iota(jnp.int32, (PACK, DEPTH), 0).astype(jnp.float32).astype(jnp.bfloat16)

    def group(g, carry):
        feats = []
        for j in range(4):
            p = g * 4 + j
            feats.append((me ^ slot_of(p // share, kind, bits)) * share + p % share)
        high = [high_ref[pl.ds(f, 1), :] for f in feats]
        low = [low_ref[pl.ds(f, 1), :] for f in feats]
        total = jnp.zeros((5 * STATS, 4 * HALF), jnp.float32)
        for k in range(rows // DEPTH):
            span = slice(k * DEPTH, (k + 1) * DEPTH)
            left = [stats_ref[:, span]]
            ladder = []
            for j in range(4):
                wide = jnp.broadcast_to(low[j][:, span], (PACK, DEPTH)).astype(jnp.bfloat16)
                for q in range(HALF // PACK):
                    reached = wide <= steps + jnp.bfloat16(PACK * q)
                    ladder.append(jnp.where(reached, jnp.bfloat16(1), jnp.bfloat16(0)))
                left.append(left[0] * jnp.broadcast_to(high[j][:, span], (STATS, DEPTH)).astype(jnp.bfloat16))
            total += lax.dot_general(
                jnp.concatenate(left, 0), jnp.concatenate(ladder, 0), NT, preferred_element_type=jnp.float32
            )
        for j in range(4):
            columns = slice(HALF * j, HALF * (j + 1))
            upper = total[STATS * (j + 1) : STATS * (j + 2), columns]
            lower = total[:STATS, columns] - upper
            out_ref[g * 4 + j] = jnp.concatenate([lower, lower[:, HALF - 1 :] + upper], 1)
        return carry

    lax.fori_loop(0, out_ref.shape[0] // 4, group, 0, unroll=2)


def first_kernel(bits, share, bins, leaf, treated, gradient, hessian, high_ref, low_ref, stats_ref, out_ref, *scratch):
    held, sems = scratch[:-1], scratch[-1]
    copies = [
        pltpu.make_async_copy(src, dst, sems.at[i])
        for i, (src, dst) in enumerate(zip((leaf, treated, gradient, hessian, bins), held))
    ]
    for copy in copies:
        copy.start()
    for copy in copies[:4]:
        copy.wait()
    stats_of(held[0][...], held[1][...], held[2][...], held[3][...], stats_ref)
    copies[4].wait()
    turned = held[4][...].T
    high_ref[...] = (turned // HALF).astype(jnp.float32)
    low_ref[...] = (turned % HALF).astype(jnp.float32)
    left_sums_of(lax.axis_index("row"), "core", bits, share, high_ref, low_ref, stats_ref, out_ref)


def next_kernel(kind, bits, share, high_ref, low_ref, stats_ref, out_ref):
    left_sums_of(lax.axis_index("row"), kind, bits, share, high_ref, low_ref, stats_ref, out_ref)


def score_of(grad_t, hess_t, grad_c, hess_c):
    value_t = grad_t / (hess_t + 1.0)
    value_c = grad_c / (hess_c + 1.0)
    spread = value_t - value_c
    return grad_t * value_t + grad_c * value_c + (hess_t + hess_c) * spread * spread


def gain_kernel(kept_ref, came_ref, gain_ref, most_ref):
    lane = lax.broadcasted_iota(jnp.int32, most_ref.shape, 1)
    most = jnp.zeros(most_ref.shape, jnp.float32)
    for leaf in range(LEAVES):
        left = [
            kept_ref[:, s * LEAVES + leaf, :] + came_ref[:, s * LEAVES + leaf, :] for s in range(4)
        ]
        parent = [jnp.broadcast_to(x[:, BINS - 1 :], x.shape) for x in left]
        right = [p - x for p, x in zip(parent, left)]
        gain = score_of(*left) + score_of(*right) - score_of(*parent)
        gain_ref[leaf] = gain
        most = jnp.where(lane == leaf, jnp.max(gain), most)
    most_ref[...] = most


VMEM = pl.BlockSpec(memory_space=pltpu.VMEM)
ANY = pl.BlockSpec(memory_space=pl.ANY)
ROOM = pltpu.CompilerParams(vmem_limit_bytes=32 * 2**20)


def body(devices, bin_values, leaf_ids, treated, gradient, hessian):
    rows, feats = bin_values.shape
    ring = lax.axis_size("row")
    bits = ring.bit_length() - 1
    share = feats // ring
    f32 = jnp.float32
    small = (rows // 128, 128)

    def work(count):
        return pl.CostEstimate(
            flops=2 * rows * count * BINS * STATS * 2, bytes_accessed=rows * count * 8, transcendentals=0
        )

    high, low, stats, core_part = pl.pallas_call(
        functools.partial(first_kernel, bits, share),
        out_shape=(
            jax.ShapeDtypeStruct((feats, rows), f32),
            jax.ShapeDtypeStruct((feats, rows), f32),
            jax.ShapeDtypeStruct((STATS, rows), jnp.bfloat16),
            jax.ShapeDtypeStruct((feats // 2, STATS, BINS), f32),
        ),
        in_specs=[ANY] * 5,
        out_specs=(VMEM,) * 4,
        scratch_shapes=[
            pltpu.VMEM(small, jnp.int32),
            pltpu.VMEM(small, jnp.int32),
            pltpu.VMEM(small, jnp.bfloat16),
            pltpu.VMEM(small, jnp.bfloat16),
            pltpu.VMEM((rows, feats), jnp.int32),
            pltpu.SemaphoreType.DMA((5,)),
        ],
        compiler_params=ROOM,
        cost_estimate=work(feats // 2),
        name="stats_and_core_part",
    )(bin_values, *(x.reshape(small) for x in (leaf_ids, treated, gradient, hessian)))

    def part(kind):
        return pl.pallas_call(
            functools.partial(next_kernel, kind, bits, share),
            out_shape=jax.ShapeDtypeStruct((feats // 4, STATS, BINS), f32),
            in_specs=[VMEM] * 3,
            out_specs=VMEM,
            compiler_params=ROOM,
            cost_estimate=work(feats // 4),
            name=kind + "_part",
        )(high, low, stats)

    def swap(x, bit):
        return lax.ppermute(x, "row", [(i, i ^ bit) for i in range(ring)])

    core_came = swap(core_part, 1)
    far = part("far")
    near = part("near")
    half = feats // 4
    far_came = swap(far + core_came[half:], 2)
    kept = near + core_came[:half]
    came = far_came
    for stage in range(2, bits):
        half = half // 2
        sent = kept[half:] + came[half:]
        kept = kept[:half] + came[:half]
        came = swap(sent, 1 << stage)

    split_gain, most = pl.pallas_call(
        gain_kernel,
        out_shape=(
            jax.ShapeDtypeStruct((LEAVES, share, BINS), f32),
            jax.ShapeDtypeStruct((devices, BINS), f32),
        ),
        in_specs=[VMEM] * 2,
        out_specs=(VMEM,) * 2,
        name="gains",
    )(kept, came)
    best = lax.all_to_all(most, ("feat", "row"), 0, 0, tiled=True)
    return split_gain, jnp.max(best, axis=0)[:LEAVES]


def solution(mesh):
    in_specs = (P("row", "feat"), P("row"), P("row"), P("row"), P("row"))
    out_specs = (P(None, ("feat", "row"), None), P())
    return jax.shard_map(
        functools.partial(body, mesh.size), mesh=mesh, in_specs=in_specs, out_specs=out_specs, check_vma=False
    )
```

```python
import functools

import jax
import jax.numpy as jnp
from jax import lax
from jax.experimental import pallas as pl
from jax.experimental.pallas import tpu as pltpu
from jax.sharding import PartitionSpec as P

BINS = 128
LEAVES = 4
STATS = 4 * LEAVES
PACK = 16
HIGH = 4
LOW = BINS // HIGH
GROUP = 8
DEPTH = 256
NT = (((1,), (1,)), ((), ()))
F32, BF16 = jnp.float32, jnp.bfloat16


def reversed_bits(value, bits):
    out = 0
    for i in range(bits):
        out = out + (((value >> i) & 1) << (bits - 1 - i))
    return out


def slot_of(position, far, other, bits):
    return reversed_bits(position, bits - 2) * 4 + 2 * far + other


def stats_of(leaf, treated, gradient, hessian, stats_ref):
    row = lax.broadcasted_iota(jnp.int32, (STATS, 128), 0)
    stat, own_leaf = row // LEAVES, row % LEAVES
    grad, hess = gradient.astype(F32), hessian.astype(F32)
    for i in range(leaf.shape[0]):
        wide = lambda x: jnp.broadcast_to(x[i : i + 1], (STATS, 128))
        value = jnp.where(stat % 2 == 0, wide(grad), wide(hess))
        ok = (wide(leaf) == own_leaf) & ((wide(treated) == 1) == (stat < 2))
        stats_ref[:, i * 128 : (i + 1) * 128] = jnp.where(ok, value, 0.0).astype(BF16)


def left_sums_of(me, far, other, bits, share, bins_ref, low_ref, stats_ref, out_ref):
    rows = bins_ref.shape[1]
    steps = lax.broadcasted_iota(jnp.int32, (PACK, DEPTH), 0).astype(F32).astype(BF16)
    one, zero = BF16(1), BF16(0)
    for g in range(out_ref.shape[0] // GROUP):
        feats = []
        for p in range(g * GROUP, (g + 1) * GROUP):
            feats.append((me ^ slot_of(p // share, far, other, bits)) * share + p % share)
        bins = [bins_ref[pl.ds(f, 1), :] for f in feats]
        low = [low_ref[pl.ds(f, 1), :] for f in feats]
        total = jnp.zeros((STATS * (1 + (HIGH - 1) * GROUP), LOW * GROUP), F32)
        for k in range(rows // DEPTH):
            span = slice(k * DEPTH, (k + 1) * DEPTH)
            stats = stats_ref[:, span]
            streamed, ladder = [stats], []
            for j in range(GROUP):
                wide = jnp.broadcast_to(low[j][:, span], (PACK, DEPTH)).astype(BF16)
                for q in range(LOW // PACK):
                    ladder.append(jnp.where(wide <= steps + BF16(PACK * q), one, zero))
                wide = jnp.broadcast_to(bins[j][:, span], (STATS, DEPTH)).astype(BF16)
                for q in range(1, HIGH):
                    streamed.append(jnp.where(wide >= BF16(LOW * q), stats, zero))
            total += lax.dot_general(
                jnp.concatenate(streamed, 0), jnp.concatenate(ladder, 0), NT, preferred_element_type=F32
            )
        for j in range(GROUP):
            columns = slice(LOW * j, LOW * (j + 1))
            reached = [total[:STATS, columns]]
            for q in range(1, HIGH):
                first = STATS * (1 + (HIGH - 1) * j + q - 1)
                reached.append(total[first : first + STATS, columns])
            pieces = []
            for q in range(HIGH):
                piece = reached[q]
                if q + 1 < HIGH:
                    piece = piece - reached[q + 1]
                if q:
                    piece = piece + (reached[0][:, LOW - 1 :] - reached[q][:, LOW - 1 :])
                pieces.append(piece)
            out_ref[g * GROUP + j] = jnp.concatenate(pieces, 1)


def first_kernel(bits, share, bins, leaf, treated, gradient, hessian, bins_ref, low_ref, stats_ref, out_ref, *scratch):
    held, sems = scratch[:-1], scratch[-1]
    copies = [
        pltpu.make_async_copy(src, dst, sems.at[i])
        for i, (src, dst) in enumerate(zip((bins, leaf, treated, gradient, hessian), held))
    ]
    for copy in copies:
        copy.start()
    for copy in copies[1:]:
        copy.wait()
    stats_of(*(ref[...] for ref in held[1:]), stats_ref)
    copies[0].wait()
    turned = held[0][...].T
    bins_ref[...] = turned.astype(F32)
    low_ref[...] = (turned % LOW).astype(F32)
    left_sums_of(lax.axis_index("row"), 1, 1, bits, share, bins_ref, low_ref, stats_ref, out_ref)


def next_kernel(far, other, bits, share, bins_ref, low_ref, stats_ref, after_ref, out_ref):
    left_sums_of(lax.axis_index("row"), far, other, bits, share, bins_ref, low_ref, stats_ref, out_ref)


def score_of(grad_t, hess_t, grad_c, hess_c):
    value_t = grad_t / (hess_t + 1.0)
    value_c = grad_c / (hess_c + 1.0)
    spread = value_t - value_c
    return grad_t * value_t + grad_c * value_c + (hess_t + hess_c) * spread * spread


def gain_kernel(kept_ref, came_ref, gain_ref, most_ref):
    tops = []
    for leaf in range(LEAVES):
        left = [kept_ref[:, s * LEAVES + leaf, :] + came_ref[:, s * LEAVES + leaf, :] for s in range(4)]
        parent = [jnp.broadcast_to(x[:, BINS - 1 :], x.shape) for x in left]
        right = [p - x for p, x in zip(parent, left)]
        gain = score_of(*left) + score_of(*right) - score_of(*parent)
        gain_ref[leaf] = gain
        tops.append(jnp.max(gain, axis=0, keepdims=True))
    top = jnp.max(jnp.concatenate(tops, 0), axis=1, keepdims=True)
    lane = lax.broadcasted_iota(jnp.int32, (LEAVES, BINS), 1)
    leaf = lax.broadcasted_iota(jnp.int32, (LEAVES, BINS), 0)
    line = jnp.sum(jnp.where(lane == leaf, top, 0.0), axis=0, keepdims=True)
    most_ref[...] = jnp.broadcast_to(line, most_ref.shape)


VMEM = pl.BlockSpec(memory_space=pltpu.VMEM)
HBM = pl.BlockSpec(memory_space=pltpu.HBM)
ANY = pl.BlockSpec(memory_space=pl.ANY)
ROOM = pltpu.CompilerParams(vmem_limit_bytes=32 * 2**20)


def body(devices, bin_values, leaf_ids, treated, gradient, hessian):
    rows, feats = bin_values.shape
    ring = lax.axis_size("row")
    bits = ring.bit_length() - 1
    share = feats // ring
    small = (rows // 128, 128)
    part = jax.ShapeDtypeStruct((feats // 4, STATS, BINS), F32)
    cost = pl.CostEstimate(
        flops=2 * rows * feats // 4 * BINS * STATS * 4, bytes_accessed=rows * feats * 2, transcendentals=0
    )

    bins, low, stats, far_other = pl.pallas_call(
        functools.partial(first_kernel, bits, share),
        out_shape=(
            jax.ShapeDtypeStruct((feats, rows), F32),
            jax.ShapeDtypeStruct((feats, rows), F32),
            jax.ShapeDtypeStruct((STATS, rows), BF16),
            part,
        ),
        in_specs=[HBM] * 5,
        out_specs=(VMEM,) * 4,
        scratch_shapes=[
            pltpu.VMEM((rows, feats), jnp.int32),
            pltpu.VMEM(small, jnp.int32),
            pltpu.VMEM(small, jnp.int32),
            pltpu.VMEM(small, BF16),
            pltpu.VMEM(small, BF16),
            pltpu.SemaphoreType.DMA((5,)),
        ],
        compiler_params=ROOM,
        cost_estimate=cost,
        name="stats_and_far_other",
    )(bin_values, *(x.reshape(small) for x in (leaf_ids, treated, gradient, hessian)))

    def left_sums(far, other, after):
        return pl.pallas_call(
            functools.partial(next_kernel, far, other, bits, share),
            out_shape=part,
            in_specs=[VMEM] * 3 + [ANY],
            out_specs=VMEM,
            compiler_params=ROOM,
            cost_estimate=cost,
            name=("near_", "far_")[far] + ("own", "other")[other],
        )(bins, low, stats, after)

    def swap(x, bit):
        return lax.ppermute(x, "row", [(i, i ^ bit) for i in range(ring)])

    far_core = swap(far_other, 1)
    far = left_sums(1, 0, far_other) + far_core
    came = swap(far, 2)
    near_other = left_sums(0, 1, far)
    near_core = swap(near_other, 1)
    kept = left_sums(0, 0, near_other) + near_core
    half = feats // 4
    for stage in range(2, bits):
        half = half // 2
        sent = kept[half:] + came[half:]
        kept = kept[:half] + came[:half]
        came = swap(sent, 1 << stage)

    split_gain, most = pl.pallas_call(
        gain_kernel,
        out_shape=(
            jax.ShapeDtypeStruct((LEAVES, share, BINS), F32),
            jax.ShapeDtypeStruct((devices, BINS), F32),
        ),
        in_specs=[VMEM] * 2,
        out_specs=(VMEM,) * 2,
        name="gains",
    )(kept, came)
    best = lax.all_to_all(most, ("feat", "row"), 0, 0, tiled=True)
    return split_gain, jnp.max(best, axis=0)[:LEAVES]


def solution(mesh):
    in_specs = (P("row", "feat"), P("row"), P("row"), P("row"), P("row"))
    out_specs = (P(None, ("feat", "row"), None), P())
    return jax.shard_map(
        functools.partial(body, mesh.size), mesh=mesh, in_specs=in_specs, out_specs=out_specs, check_vma=False
    )
```

```python
import functools

import jax
import jax.numpy as jnp
from jax import lax
from jax.experimental import pallas as pl
from jax.experimental.pallas import tpu as pltpu
from jax.sharding import PartitionSpec as P

BINS = 128
LEAVES = 4
STATS = 4 * LEAVES
PACK = 16
HIGH = 4
LOW = BINS // HIGH
GROUP = 8
DEPTH = 256
NT = (((1,), (1,)), ((), ()))
F32, BF16 = jnp.float32, jnp.bfloat16


def reversed_bits(value, bits):
    return sum(((value >> i) & 1) << (bits - 1 - i) for i in range(bits))


def slots_of(bits, fixed, free):
    later = range(1 << (bits - 3))
    return [fixed + free * upper + 8 * reversed_bits(i, bits - 3) for upper in (0, 1) for i in later]


def features_of(bits, share, core, chunk):
    one = [(s, j) for s in slots_of(bits, core + 2 * chunk, 4) for j in range(share // 2)]
    two = [(s, j) for s in slots_of(bits, core + 4 * chunk, 2) for j in range(share // 2, share)]
    return one + two


def stats_of(columns_ref, stats_ref):
    row = lax.broadcasted_iota(jnp.int32, (STATS, 128), 0)
    stat, own_leaf = row // LEAVES, (row % LEAVES).astype(F32)
    blocks = columns_ref.shape[0] // 4
    for i in range(blocks):
        leaf, treated, grad, hess = (
            jnp.broadcast_to(columns_ref[c * blocks + i : c * blocks + i + 1, :], (STATS, 128)) for c in range(4)
        )
        value = jnp.where(stat % 2 == 0, grad, hess)
        ok = (leaf == own_leaf) & ((treated == 1.0) == (stat < 2))
        stats_ref[:, i * 128 : (i + 1) * 128] = jnp.where(ok, value, 0.0).astype(BF16)


def left_sums_of(me, features, share, bins_ref, low_ref, stats_ref, out_ref):
    rows = bins_ref.shape[1]
    steps = lax.broadcasted_iota(jnp.int32, (PACK, DEPTH), 0).astype(F32).astype(BF16)
    one, zero = BF16(1), BF16(0)
    for g in range(out_ref.shape[0] // GROUP):
        feats = [(me ^ slot) * share + j for slot, j in features[g * GROUP : (g + 1) * GROUP]]
        bins = [bins_ref[pl.ds(f, 1), :] for f in feats]
        low = [low_ref[pl.ds(f, 1), :] for f in feats]
        total = jnp.zeros((STATS * (1 + (HIGH - 1) * GROUP), LOW * GROUP), F32)
        for k in range(rows // DEPTH):
            span = slice(k * DEPTH, (k + 1) * DEPTH)
            stats = stats_ref[:, span]
            streamed, ladder = [stats], []
            for j in range(GROUP):
                wide = jnp.broadcast_to(low[j][:, span], (PACK, DEPTH)).astype(BF16)
                for q in range(LOW // PACK):
                    ladder.append(jnp.where(wide <= steps + BF16(PACK * q), one, zero))
                wide = jnp.broadcast_to(bins[j][:, span], (STATS, DEPTH)).astype(BF16)
                for q in range(1, HIGH):
                    streamed.append(jnp.where(wide >= BF16(LOW * q), stats, zero))
            total += lax.dot_general(
                jnp.concatenate(streamed, 0), jnp.concatenate(ladder, 0), NT, preferred_element_type=F32
            )
        for j in range(GROUP):
            columns = slice(LOW * j, LOW * (j + 1))
            reached = [total[:STATS, columns]]
            for q in range(1, HIGH):
                first = STATS * (1 + (HIGH - 1) * j + q - 1)
                reached.append(total[first : first + STATS, columns])
            pieces = []
            for q in range(HIGH):
                piece = reached[q]
                if q + 1 < HIGH:
                    piece = piece - reached[q + 1]
                if q:
                    piece = piece + (reached[0][:, LOW - 1 :] - reached[q][:, LOW - 1 :])
                pieces.append(piece)
            out_ref[g * GROUP + j] = jnp.concatenate(pieces, 1)


def first_kernel(features, share, columns, bins, bins_ref, low_ref, stats_ref, out_ref):
    stats_of(columns, stats_ref)
    turned = bins[...].T
    bins_ref[...] = turned.astype(F32)
    low_ref[...] = (turned % LOW).astype(F32)
    left_sums_of(lax.axis_index("row"), features, share, bins_ref, low_ref, stats_ref, out_ref)


def next_kernel(features, share, bins_ref, low_ref, stats_ref, *refs):
    left_sums_of(lax.axis_index("row"), features, share, bins_ref, low_ref, stats_ref, refs[-1])


def score_of(grad_t, hess_t, grad_c, hess_c):
    value_t = grad_t / (hess_t + 1.0)
    value_c = grad_c / (hess_c + 1.0)
    spread = value_t - value_c
    return grad_t * value_t + grad_c * value_c + (hess_t + hess_c) * spread * spread


def gain_kernel(kept_ref, came_ref, gain_ref, most_ref):
    tops = []
    for leaf in range(LEAVES):
        left = [kept_ref[:, s * LEAVES + leaf, :] + came_ref[:, s * LEAVES + leaf, :] for s in range(4)]
        parent = [jnp.broadcast_to(x[:, BINS - 1 :], x.shape) for x in left]
        right = [p - x for p, x in zip(parent, left)]
        gain = score_of(*left) + score_of(*right) - score_of(*parent)
        gain_ref[leaf] = gain
        tops.append(jnp.max(gain, axis=0, keepdims=True))
    top = jnp.max(jnp.concatenate(tops, 0), axis=1, keepdims=True)
    lane = lax.broadcasted_iota(jnp.int32, (LEAVES, BINS), 1)
    leaf = lax.broadcasted_iota(jnp.int32, (LEAVES, BINS), 0)
    line = jnp.sum(jnp.where(lane == leaf, top, 0.0), axis=0, keepdims=True)
    most_ref[...] = jnp.broadcast_to(line, most_ref.shape)


VMEM = pl.BlockSpec(memory_space=pltpu.VMEM)
ANY = pl.BlockSpec(memory_space=pl.ANY)
ROOM = pltpu.CompilerParams(vmem_limit_bytes=32 * 2**20)


def body(devices, bin_values, leaf_ids, treated, gradient, hessian):
    rows, feats = bin_values.shape
    ring = lax.axis_size("row")
    bits = ring.bit_length() - 1
    share = feats // ring
    part = jax.ShapeDtypeStruct((feats // 4, STATS, BINS), F32)
    cost = pl.CostEstimate(flops=rows * feats, bytes_accessed=rows * feats // 4, transcendentals=0)

    columns = jnp.concatenate([x.astype(F32) for x in (leaf_ids, treated, gradient, hessian)])
    bins, low, stats, other = pl.pallas_call(
        functools.partial(first_kernel, features_of(bits, share, 1, 1), share),
        out_shape=(
            jax.ShapeDtypeStruct((feats, rows), F32),
            jax.ShapeDtypeStruct((feats, rows), F32),
            jax.ShapeDtypeStruct((STATS, rows), BF16),
            part,
        ),
        in_specs=[VMEM] * 2,
        out_specs=(VMEM,) * 4,
        compiler_params=ROOM,
        cost_estimate=cost,
        name="stats_and_first_other",
    )(columns.reshape(4 * rows // 128, 128), bin_values)

    def left_sums(core, chunk, *after):
        return pl.pallas_call(
            functools.partial(next_kernel, features_of(bits, share, core, chunk), share),
            out_shape=part,
            in_specs=[VMEM] * 3 + [ANY] * len(after),
            out_specs=VMEM,
            compiler_params=ROOM,
            cost_estimate=cost,
            name=("second_", "first_")[chunk] + ("own", "other")[core],
        )(bins, low, stats, *after)

    def swap(x, mask):
        return lax.ppermute(x, "row", [(i, i ^ mask) for i in range(ring)])

    def halves(x):
        return x[: x.shape[0] // 2], x[x.shape[0] // 2 :]

    came = swap(other, 1)
    one, two = (x + y for x, y in zip(halves(left_sums(0, 1, other)), halves(came)))
    other = left_sums(1, 0, one, two)
    came_one, came_two = swap(one, 2), swap(two, 4)
    came = swap(other, 1)
    one, two = halves(left_sums(0, 0, other))
    one, two = lax.optimization_barrier((one + came_one, two + came_two))
    came_one, came_two = halves(came)
    (one, far_one), (two, far_two) = ([a + b for a, b in zip(halves(x), halves(y))] for x, y in ((one, came_one), (two, came_two)))
    came_one, came_two = swap(far_one, 4), swap(far_two, 2)

    def joined(one, two):
        pieces = [x.reshape(-1, share // 2, STATS, BINS) for x in (one, two)]
        return jnp.concatenate(pieces, 1).reshape(-1, STATS, BINS)

    kept, came = joined(one, two), joined(came_one, came_two)
    for stage in range(3, bits):
        (kept, sent), (came, came_sent) = halves(kept), halves(came)
        kept, came = kept + came, swap(sent + came_sent, 1 << stage)

    split_gain, most = pl.pallas_call(
        gain_kernel,
        out_shape=(
            jax.ShapeDtypeStruct((LEAVES, share, BINS), F32),
            jax.ShapeDtypeStruct((devices, BINS), F32),
        ),
        in_specs=[VMEM] * 2,
        out_specs=(VMEM,) * 2,
        compiler_params=ROOM,
        name="gains",
    )(kept, came)
    best = lax.all_to_all(most, ("feat", "row"), 0, 0, tiled=True)
    return split_gain, jnp.max(best, axis=0)[:LEAVES]


def solution(mesh):
    in_specs = (P("row", "feat"), P("row"), P("row"), P("row"), P("row"))
    out_specs = (P(None, ("feat", "row"), None), P())
    return jax.shard_map(
        functools.partial(body, mesh.size), mesh=mesh, in_specs=in_specs, out_specs=out_specs, check_vma=False
    )
```

```python
import functools

import jax
import jax.numpy as jnp
from jax import lax
from jax.experimental import pallas as pl
from jax.experimental.pallas import tpu as pltpu
from jax.sharding import PartitionSpec as P

BINS = 128
LEAVES = 4
STATS = 4 * LEAVES
PACK = 16
HIGH = 4
LOW = BINS // HIGH
GROUP = 8
DEPTH = 256
BLOCKS = 2
NT = (((1,), (1,)), ((), ()))
F32, BF16 = jnp.float32, jnp.bfloat16


def reversed_bits(value, bits):
    return sum(((value >> i) & 1) << (bits - 1 - i) for i in range(bits))


def features_of(bits, share, core, *nears):
    out = []
    for near in nears:
        slots = [core + 2 * near + 8 * reversed_bits(i, bits - 3) for i in range(1 << (bits - 3))]
        for half in (range(share // 2), range(share // 2, share)):
            out += [(s, j) for s in slots for j in half]
    return out


def stats_of(leaf_ref, treated_ref, gradient_ref, hessian_ref, stats_ref):
    row = lax.broadcasted_iota(jnp.int32, (STATS, 128), 0)
    stat, own_leaf = row // LEAVES, row % LEAVES
    gradient, hessian = gradient_ref[...].astype(F32), hessian_ref[...].astype(F32)
    for i in range(leaf_ref.shape[0]):
        wide = lambda x: jnp.broadcast_to(x[i : i + 1, :], (STATS, 128))
        value = jnp.where(stat % 2 == 0, wide(gradient), wide(hessian))
        ok = (wide(leaf_ref) == own_leaf) & ((wide(treated_ref) == 1) == (stat < 2))
        stats_ref[:, i * 128 : (i + 1) * 128] = jnp.where(ok, value, 0.0).astype(BF16)


def left_sums_of(me, features, share, bins_ref, low_ref, stats_ref, out_ref):
    rows = bins_ref.shape[1]
    steps = lax.broadcasted_iota(jnp.int32, (PACK, DEPTH), 0).astype(F32).astype(BF16)
    one, zero = BF16(1), BF16(0)
    for g in range(out_ref.shape[0] // GROUP):
        feats = [(me ^ slot) * share + j for slot, j in features[g * GROUP : (g + 1) * GROUP]]
        bins = [bins_ref[pl.ds(f, 1), :] for f in feats]
        low = [low_ref[pl.ds(f, 1), :] for f in feats]
        total = jnp.zeros((STATS * (1 + (HIGH - 1) * GROUP), LOW * GROUP), F32)
        for k in range(rows // DEPTH):
            span = slice(k * DEPTH, (k + 1) * DEPTH)
            stats = stats_ref[:, span]
            streamed, ladder = [stats], []
            for j in range(GROUP):
                wide = jnp.broadcast_to(low[j][:, span], (PACK, DEPTH)).astype(BF16)
                for q in range(LOW // PACK):
                    ladder.append(jnp.where(wide <= steps + BF16(PACK * q), one, zero))
                wide = jnp.broadcast_to(bins[j][:, span], (STATS, DEPTH)).astype(BF16)
                for q in range(1, HIGH):
                    streamed.append(jnp.where(wide >= BF16(LOW * q), stats, zero))
            total += lax.dot_general(
                jnp.concatenate(streamed, 0), jnp.concatenate(ladder, 0), NT, preferred_element_type=F32
            )
        for j in range(GROUP):
            columns = slice(LOW * j, LOW * (j + 1))
            reached = [total[:STATS, columns]]
            for q in range(1, HIGH):
                first = STATS * (1 + (HIGH - 1) * j + q - 1)
                reached.append(total[first : first + STATS, columns])
            pieces = []
            for q in range(HIGH):
                piece = reached[q]
                if q + 1 < HIGH:
                    piece = piece - reached[q + 1]
                pieces.append(piece)
            out_ref[g * GROUP + j] = jnp.concatenate(pieces, 1)


def first_kernel(features, share, bins, leaf, treated, gradient, hessian, bins_ref, low_ref, stats_ref, out_ref, *scratch):
    columns, held, sems = scratch[:4], scratch[4], scratch[5]
    small = [
        pltpu.make_async_copy(src, dst, sems.at[i]) for i, (src, dst) in enumerate(zip((leaf, treated, gradient, hessian), columns))
    ]
    blocks = [slice(i, i + held.shape[0] // BLOCKS) for i in range(0, held.shape[0], held.shape[0] // BLOCKS)]
    large = [pltpu.make_async_copy(bins.at[rows], held.at[rows], sems.at[4 + i]) for i, rows in enumerate(blocks)]
    for copy in large + small:
        copy.start()
    for copy, rows in zip(large, blocks):
        copy.wait()
        turned = held[rows].T
        bins_ref[:, rows] = turned.astype(F32)
        low_ref[:, rows] = (turned & (LOW - 1)).astype(F32)
    for copy in small:
        copy.wait()
    stats_of(*columns, stats_ref)
    left_sums_of(lax.axis_index("row"), features, share, bins_ref, low_ref, stats_ref, out_ref)


def next_kernel(features, share, bins_ref, low_ref, stats_ref, *refs):
    left_sums_of(lax.axis_index("row"), features, share, bins_ref, low_ref, stats_ref, refs[-1])


def score_of(grad_t, hess_t, grad_c, hess_c):
    value_t = grad_t / (hess_t + 1.0)
    value_c = grad_c / (hess_c + 1.0)
    spread = value_t - value_c
    return grad_t * value_t + grad_c * value_c + (hess_t + hess_c) * spread * spread


def gain_kernel(kept_ref, came_ref, gain_ref, most_ref, sums_ref, parent_ref):
    share = gain_ref.shape[1]
    x = (kept_ref[...] + came_ref[...]).reshape(share * STATS, BINS)
    source = lax.broadcasted_iota(jnp.int32, (BINS, 2 * BINS), 0)
    target = lax.broadcasted_iota(jnp.int32, (BINS, 2 * BINS), 1)
    carried = (source % LOW == LOW - 1) & ((target >= BINS) | (source // LOW < target // LOW))
    carried = jnp.where(carried, 1.0, 0.0).astype(BF16)
    carry, rest = 0.0, x
    for _ in range(3):
        piece = rest.astype(BF16)
        rest = rest - piece.astype(F32)
        carry = carry + jnp.dot(piece, carried, preferred_element_type=F32)
    sums_ref[...] = (x + carry[:, :BINS]).reshape(sums_ref.shape)
    parent_ref[...] = carry[:, BINS:].reshape(parent_ref.shape)
    tops = []
    for leaf in range(LEAVES):
        left = [sums_ref[:, s * LEAVES + leaf, :] for s in range(4)]
        parent = [parent_ref[:, s * LEAVES + leaf, :] for s in range(4)]
        right = [p - x for p, x in zip(parent, left)]
        gain = score_of(*left) + score_of(*right) - score_of(*parent)
        gain_ref[leaf] = gain
        tops.append(jnp.max(gain, axis=0, keepdims=True))
    top = jnp.max(jnp.concatenate(tops, 0), axis=1, keepdims=True)
    lane = lax.broadcasted_iota(jnp.int32, (LEAVES, BINS), 1)
    leaf = lax.broadcasted_iota(jnp.int32, (LEAVES, BINS), 0)
    line = jnp.sum(jnp.where(lane == leaf, top, 0.0), axis=0, keepdims=True)
    most_ref[...] = jnp.broadcast_to(line, most_ref.shape)


VMEM = pl.BlockSpec(memory_space=pltpu.VMEM)
HBM = pl.BlockSpec(memory_space=pltpu.HBM)
ANY = pl.BlockSpec(memory_space=pl.ANY)
ROOM = pltpu.CompilerParams(vmem_limit_bytes=32 * 2**20)


def body(devices, bin_values, leaf_ids, treated, gradient, hessian):
    rows, feats = bin_values.shape
    ring = lax.axis_size("row")
    bits = ring.bit_length() - 1
    share = feats // ring
    size = feats // 8
    cost = pl.CostEstimate(flops=rows * feats, bytes_accessed=rows * feats // 4, transcendentals=0)

    small = (rows // 128, 128)
    inputs = (bin_values, *(x.reshape(small) for x in (leaf_ids, treated, gradient, hessian)))
    bins, low, stats, other = pl.pallas_call(
        functools.partial(first_kernel, features_of(bits, share, 1, 3), share),
        out_shape=(
            jax.ShapeDtypeStruct((feats, rows), F32),
            jax.ShapeDtypeStruct((feats, rows), F32),
            jax.ShapeDtypeStruct((STATS, rows), BF16),
            jax.ShapeDtypeStruct((size, STATS, BINS), F32),
        ),
        in_specs=[HBM] * 5,
        out_specs=(VMEM,) * 4,
        scratch_shapes=[
            pltpu.VMEM(small, jnp.int32),
            pltpu.VMEM(small, jnp.int32),
            pltpu.VMEM(small, BF16),
            pltpu.VMEM(small, BF16),
            pltpu.VMEM((rows, feats), jnp.int32),
            pltpu.SemaphoreType.DMA((4 + BLOCKS,)),
        ],
        compiler_params=ROOM,
        cost_estimate=cost,
        name="stats_and_others",
    )(*(pltpu.with_memory_space_constraint(x, pltpu.HBM) for x in inputs))

    def left_sums(core, nears, *after):
        return pl.pallas_call(
            functools.partial(next_kernel, features_of(bits, share, core, *nears), share),
            out_shape=jax.ShapeDtypeStruct((size * len(nears), STATS, BINS), F32),
            in_specs=[VMEM] * 3 + [ANY] * len(after),
            out_specs=VMEM,
            compiler_params=ROOM,
            cost_estimate=cost,
            name="left_sums_%d_%d" % (core, len(nears) * 10 + nears[0]),
        )(bins, low, stats, *after)

    def swap(x, mask):
        return lax.ppermute(x, "row", [(i, i ^ mask) for i in range(ring)])

    def halves(x):
        return x[: x.shape[0] // 2], x[x.shape[0] // 2 :]

    came = swap(other, 1)
    one, two = (x + y for x, y in zip(halves(left_sums(0, [3], other)), halves(came)))
    other = left_sums(1, [1, 2], one, two)
    came_one, came_two = swap(one, 2), swap(two, 4)
    came = halves(swap(other, 1))
    along_one, along_two = halves(left_sums(0, [1, 2], other))
    (one_a, one_b), (two_a, two_b) = halves(along_one), halves(along_two)
    one_b, two_a = lax.optimization_barrier((one_b + came_two, two_a + came_one))
    (core_one_a, core_one_b), (core_two_a, core_two_b) = halves(came[0]), halves(came[1])
    one = jnp.concatenate([one_a + core_one_a, one_b + core_one_b])
    two = jnp.concatenate([two_a + core_two_a, two_b + core_two_b])
    other = left_sums(1, [0], one, two)
    came_one, came_two = swap(one, 2), swap(two, 4)
    came = swap(other, 1)
    kept = lax.optimization_barrier(left_sums(0, [0], other) + (came_one + came_two))

    def joined(x):
        return jnp.concatenate([y.reshape(-1, share // 2, STATS, BINS) for y in halves(x)], 1).reshape(-1, STATS, BINS)

    kept, came = joined(kept), joined(came)
    for stage in range(3, bits):
        (kept, sent), (came, came_sent) = halves(kept), halves(came)
        kept, came = kept + came, swap(sent + came_sent, 1 << stage)

    split_gain, most = pl.pallas_call(
        gain_kernel,
        out_shape=(
            jax.ShapeDtypeStruct((LEAVES, share, BINS), F32),
            jax.ShapeDtypeStruct((devices, BINS), F32),
        ),
        in_specs=[VMEM] * 2,
        out_specs=(VMEM,) * 2,
        scratch_shapes=[pltpu.VMEM((share, STATS, BINS), F32)] * 2,
        compiler_params=ROOM,
        name="gains",
    )(kept, came)
    best = lax.all_to_all(most, ("feat", "row"), 0, 0, tiled=True)
    return split_gain, jnp.max(best, axis=0)[:LEAVES]


def solution(mesh):
    in_specs = (P("row", "feat"), P("row"), P("row"), P("row"), P("row"))
    out_specs = (P(None, ("feat", "row"), None), P())
    return jax.shard_map(
        functools.partial(body, mesh.size), mesh=mesh, in_specs=in_specs, out_specs=out_specs, check_vma=False
    )
```

```python
import functools

import jax
import jax.numpy as jnp
from jax import lax
from jax.experimental import pallas as pl
from jax.experimental.pallas import tpu as pltpu
from jax.sharding import PartitionSpec as P

BINS = 128
LEAVES = 4
STATS = 4 * LEAVES
PACK = 16
HIGH = 4
LOW = BINS // HIGH
GROUP = 8
DEPTH = 256
BLOCKS = 2
NT = (((1,), (1,)), ((), ()))
F32, BF16 = jnp.float32, jnp.bfloat16


def reversed_bits(value, bits):
    return sum(((value >> i) & 1) << (bits - 1 - i) for i in range(bits))


def features_of(bits, share, core, *nears):
    slots = [core + 2 * near + 8 * reversed_bits(i, bits - 3) for near in nears for i in range(1 << (bits - 3))]
    return [(s, j) for s in slots for j in range(share)]


def stats_of(leaf_ref, treated_ref, gradient_ref, hessian_ref, stats_ref):
    row = lax.broadcasted_iota(jnp.int32, (STATS, 128), 0)
    stat, own_leaf = row // LEAVES, row % LEAVES
    gradient, hessian = gradient_ref[...].astype(F32), hessian_ref[...].astype(F32)
    for i in range(leaf_ref.shape[0]):
        wide = lambda x: jnp.broadcast_to(x[i : i + 1, :], (STATS, 128))
        value = jnp.where(stat % 2 == 0, wide(gradient), wide(hessian))
        ok = (wide(leaf_ref) == own_leaf) & ((wide(treated_ref) == 1) == (stat < 2))
        stats_ref[:, i * 128 : (i + 1) * 128] = jnp.where(ok, value, 0.0).astype(BF16)


def left_sums_of(me, features, share, bins_ref, stats_ref, out_ref):
    rows = bins_ref.shape[1]
    steps = lax.broadcasted_iota(jnp.int32, (PACK, DEPTH), 0).astype(F32).astype(BF16)
    one, zero = BF16(1), BF16(0)
    for g in range(out_ref.shape[0] // GROUP):
        feats = [(me ^ slot) * share + j for slot, j in features[g * GROUP : (g + 1) * GROUP]]
        bins = [bins_ref[pl.ds(f, 1), :] for f in feats]
        total = jnp.zeros((STATS * (1 + (HIGH - 1) * GROUP), LOW * GROUP), F32)
        for k in range(rows // DEPTH):
            span = slice(k * DEPTH, (k + 1) * DEPTH)
            stats = stats_ref[:, span]
            streamed, ladder = [stats], []
            for j in range(GROUP):
                wide = jnp.broadcast_to(bins[j][:, span], (STATS, DEPTH)).astype(BF16)
                low = wide
                for q in range(1, HIGH):
                    beyond = wide >= BF16(LOW * q)
                    streamed.append(jnp.where(beyond, stats, zero))
                    low = low - jnp.where(beyond, BF16(LOW), zero)
                for q in range(LOW // PACK):
                    ladder.append(jnp.where(low <= steps + BF16(PACK * q), one, zero))
            total += lax.dot_general(
                jnp.concatenate(streamed, 0), jnp.concatenate(ladder, 0), NT, preferred_element_type=F32
            )
        for j in range(GROUP):
            columns = slice(LOW * j, LOW * (j + 1))
            reached = [total[:STATS, columns]]
            for q in range(1, HIGH):
                first = STATS * (1 + (HIGH - 1) * j + q - 1)
                reached.append(total[first : first + STATS, columns])
            pieces = []
            for q in range(HIGH):
                piece = reached[q]
                if q + 1 < HIGH:
                    piece = piece - reached[q + 1]
                pieces.append(piece)
            out_ref[g * GROUP + j] = jnp.concatenate(pieces, 1)


def first_kernel(features, share, bins, leaf, treated, gradient, hessian, bins_ref, stats_ref, out_ref, *scratch):
    columns, held, sems = scratch[:4], scratch[4], scratch[5]
    small = [
        pltpu.make_async_copy(src, dst, sems.at[i]) for i, (src, dst) in enumerate(zip((leaf, treated, gradient, hessian), columns))
    ]
    blocks = [slice(i, i + held.shape[0] // BLOCKS) for i in range(0, held.shape[0], held.shape[0] // BLOCKS)]
    large = [pltpu.make_async_copy(bins.at[rows], held.at[rows], sems.at[4 + i]) for i, rows in enumerate(blocks)]
    for copy in large + small:
        copy.start()
    for copy, rows in zip(large, blocks):
        copy.wait()
        turned = held[rows].T
        bins_ref[:, rows] = turned.astype(F32)
    for copy in small:
        copy.wait()
    stats_of(*columns, stats_ref)
    left_sums_of(lax.axis_index("row"), features, share, bins_ref, stats_ref, out_ref)


def next_kernel(features, share, bins_ref, stats_ref, *refs):
    left_sums_of(lax.axis_index("row"), features, share, bins_ref, stats_ref, refs[-1])


def score_of(grad_t, hess_t, grad_c, hess_c):
    value_t = grad_t / (hess_t + 1.0)
    value_c = grad_c / (hess_c + 1.0)
    spread = value_t - value_c
    return grad_t * value_t + grad_c * value_c + (hess_t + hess_c) * spread * spread


def gain_kernel(kept_ref, came_ref, gain_ref, most_ref, sums_ref, parent_ref):
    share = gain_ref.shape[1]
    x = (kept_ref[...] + came_ref[...]).reshape(share * STATS, BINS)
    source = lax.broadcasted_iota(jnp.int32, (BINS, 2 * BINS), 0)
    target = lax.broadcasted_iota(jnp.int32, (BINS, 2 * BINS), 1)
    carried = (source % LOW == LOW - 1) & ((target >= BINS) | (source // LOW < target // LOW))
    carried = jnp.where(carried, 1.0, 0.0).astype(BF16)
    carry, rest = 0.0, x
    for _ in range(3):
        piece = rest.astype(BF16)
        rest = rest - piece.astype(F32)
        carry = carry + jnp.dot(piece, carried, preferred_element_type=F32)
    sums_ref[...] = (x + carry[:, :BINS]).reshape(sums_ref.shape)
    parent_ref[...] = carry[:, BINS:].reshape(parent_ref.shape)
    tops = []
    for leaf in range(LEAVES):
        left = [sums_ref[:, s * LEAVES + leaf, :] for s in range(4)]
        parent = [parent_ref[:, s * LEAVES + leaf, :] for s in range(4)]
        right = [p - x for p, x in zip(parent, left)]
        gain = score_of(*left) + score_of(*right) - score_of(*parent)
        gain_ref[leaf] = gain
        tops.append(jnp.max(gain, axis=0, keepdims=True))
    top = jnp.max(jnp.concatenate(tops, 0), axis=1, keepdims=True)
    lane = lax.broadcasted_iota(jnp.int32, (LEAVES, BINS), 1)
    leaf = lax.broadcasted_iota(jnp.int32, (LEAVES, BINS), 0)
    line = jnp.sum(jnp.where(lane == leaf, top, 0.0), axis=0, keepdims=True)
    most_ref[...] = jnp.broadcast_to(line, most_ref.shape)


VMEM = pl.BlockSpec(memory_space=pltpu.VMEM)
HBM = pl.BlockSpec(memory_space=pltpu.HBM)
ANY = pl.BlockSpec(memory_space=pl.ANY)
ROOM = pltpu.CompilerParams(vmem_limit_bytes=32 * 2**20)


def body(devices, bin_values, leaf_ids, treated, gradient, hessian):
    rows, feats = bin_values.shape
    ring = lax.axis_size("row")
    bits = ring.bit_length() - 1
    share = feats // ring
    size = feats // 8
    cost = pl.CostEstimate(flops=rows * feats, bytes_accessed=rows * feats // 4, transcendentals=0)

    small = (rows // 128, 128)
    inputs = (bin_values, *(x.reshape(small) for x in (leaf_ids, treated, gradient, hessian)))
    bins, stats, other = pl.pallas_call(
        functools.partial(first_kernel, features_of(bits, share, 1, 3), share),
        out_shape=(
            jax.ShapeDtypeStruct((feats, rows), F32),
            jax.ShapeDtypeStruct((STATS, rows), BF16),
            jax.ShapeDtypeStruct((size, STATS, BINS), F32),
        ),
        in_specs=[HBM] * 5,
        out_specs=(VMEM,) * 3,
        scratch_shapes=[
            pltpu.VMEM(small, jnp.int32),
            pltpu.VMEM(small, jnp.int32),
            pltpu.VMEM(small, BF16),
            pltpu.VMEM(small, BF16),
            pltpu.VMEM((rows, feats), jnp.int32),
            pltpu.SemaphoreType.DMA((4 + BLOCKS,)),
        ],
        compiler_params=ROOM,
        cost_estimate=cost,
        name="stats_and_others",
    )(*(pltpu.with_memory_space_constraint(x, pltpu.HBM) for x in inputs))

    def left_sums(core, nears, *after):
        return pl.pallas_call(
            functools.partial(next_kernel, features_of(bits, share, core, *nears), share),
            out_shape=jax.ShapeDtypeStruct((size * len(nears), STATS, BINS), F32),
            in_specs=[VMEM] * 2 + [ANY] * len(after),
            out_specs=VMEM,
            compiler_params=ROOM,
            cost_estimate=cost,
            name="left_sums_%d_%d" % (core, len(nears) * 10 + nears[0]),
        )(bins, stats, *after)

    def swap(x, mask):
        return lax.ppermute(x, "row", [(i, i ^ mask) for i in range(ring)])

    def halves(x):
        return x[: x.shape[0] // 2], x[x.shape[0] // 2 :]

    came = swap(other, 1)
    diagonal = left_sums(0, [3], other) + came
    other = left_sums(1, [1, 2], diagonal)
    diagonal = swap(diagonal, 2)
    came = halves(swap(other, 1))
    one, two = halves(left_sums(0, [1, 2], other))
    one, two = one + came[0], lax.optimization_barrier(two + diagonal) + came[1]
    other = left_sums(1, [0], one, two)
    one, two = swap(one, 2), swap(two, 4)
    came = swap(other, 1)
    kept = lax.optimization_barrier(left_sums(0, [0], other) + (one + two))
    for stage in range(3, bits):
        (kept, sent), (came, came_sent) = halves(kept), halves(came)
        kept, came = kept + came, swap(sent + came_sent, 1 << stage)

    split_gain, most = pl.pallas_call(
        gain_kernel,
        out_shape=(
            jax.ShapeDtypeStruct((LEAVES, share, BINS), F32),
            jax.ShapeDtypeStruct((devices, BINS), F32),
        ),
        in_specs=[VMEM] * 2,
        out_specs=(VMEM,) * 2,
        scratch_shapes=[pltpu.VMEM((share, STATS, BINS), F32)] * 2,
        compiler_params=ROOM,
        name="gains",
    )(kept, came)
    best = lax.all_to_all(most, ("feat", "row"), 0, 0, tiled=True)
    return split_gain, jnp.max(best, axis=0)[:LEAVES]


def solution(mesh):
    in_specs = (P("row", "feat"), P("row"), P("row"), P("row"), P("row"))
    out_specs = (P(None, ("feat", "row"), None), P())
    return jax.shard_map(
        functools.partial(body, mesh.size), mesh=mesh, in_specs=in_specs, out_specs=out_specs, check_vma=False
    )
```

```python
import functools

import jax
import jax.numpy as jnp
from jax import lax
from jax.experimental import pallas as pl
from jax.experimental.pallas import tpu as pltpu
from jax.sharding import PartitionSpec as P

BINS = 128
LEAVES = 4
STATS = 4 * LEAVES
PACK = 16
HIGH = 4
LOW = BINS // HIGH
GROUP = 8
DEPTH = 512
BLOCKS = 2
NT = (((1,), (1,)), ((), ()))
F32, BF16 = jnp.float32, jnp.bfloat16


def reversed_bits(value, bits):
    return sum(((value >> i) & 1) << (bits - 1 - i) for i in range(bits))


def features_of(bits, share, core, *nears):
    slots = [core + 2 * near + 8 * reversed_bits(i, bits - 3) for near in nears for i in range(1 << (bits - 3))]
    return [(s, j) for s in slots for j in range(share)]


def stats_of(leaf_ref, treated_ref, gradient_ref, hessian_ref, stats_ref):
    row = lax.broadcasted_iota(jnp.int32, (STATS, 128), 0)
    stat, own_leaf = row // LEAVES, row % LEAVES
    gradient, hessian = gradient_ref[...].astype(F32), hessian_ref[...].astype(F32)
    for i in range(leaf_ref.shape[0]):
        wide = lambda x: jnp.broadcast_to(x[i : i + 1, :], (STATS, 128))
        value = jnp.where(stat % 2 == 0, wide(gradient), wide(hessian))
        ok = (wide(leaf_ref) == own_leaf) & ((wide(treated_ref) == 1) == (stat < 2))
        stats_ref[:, i * 128 : (i + 1) * 128] = jnp.where(ok, value, 0.0).astype(BF16)


def left_sums_of(me, features, share, bins_ref, stats_ref, out_ref):
    rows = bins_ref.shape[1]
    steps = lax.broadcasted_iota(jnp.int32, (PACK, DEPTH), 0).astype(F32).astype(BF16)
    one, zero = BF16(1), BF16(0)
    for g in range(out_ref.shape[0] // GROUP):
        feats = [(me ^ slot) * share + j for slot, j in features[g * GROUP : (g + 1) * GROUP]]
        bins = [bins_ref[pl.ds(f, 1), :] for f in feats]
        total = jnp.zeros((STATS * (1 + (HIGH - 1) * GROUP), LOW * GROUP), F32)
        for k in range(rows // DEPTH):
            span = slice(k * DEPTH, (k + 1) * DEPTH)
            stats = stats_ref[:, span]
            streamed, ladder = [stats], []
            for j in range(GROUP):
                wide = jnp.broadcast_to(bins[j][:, span], (STATS, DEPTH)).astype(BF16)
                low = wide
                for q in range(1, HIGH):
                    beyond = wide >= BF16(LOW * q)
                    streamed.append(jnp.where(beyond, stats, zero))
                    low = low - jnp.where(beyond, BF16(LOW), zero)
                for q in range(LOW // PACK):
                    ladder.append(jnp.where(low <= steps + BF16(PACK * q), one, zero))
            total += lax.dot_general(
                jnp.concatenate(streamed, 0), jnp.concatenate(ladder, 0), NT, preferred_element_type=F32
            )
        for j in range(GROUP):
            columns = slice(LOW * j, LOW * (j + 1))
            reached = [total[:STATS, columns]]
            for q in range(1, HIGH):
                first = STATS * (1 + (HIGH - 1) * j + q - 1)
                reached.append(total[first : first + STATS, columns])
            pieces = []
            for q in range(HIGH):
                piece = reached[q]
                if q + 1 < HIGH:
                    piece = piece - reached[q + 1]
                pieces.append(piece)
            out_ref[g * GROUP + j] = jnp.concatenate(pieces, 1)


def first_kernel(features, share, bins, leaf, treated, gradient, hessian, bins_ref, stats_ref, out_ref, *scratch):
    columns, held, sems = scratch[:4], scratch[4], scratch[5]
    small = [
        pltpu.make_async_copy(src, dst, sems.at[i]) for i, (src, dst) in enumerate(zip((leaf, treated, gradient, hessian), columns))
    ]
    blocks = [slice(i, i + held.shape[0] // BLOCKS) for i in range(0, held.shape[0], held.shape[0] // BLOCKS)]
    large = [pltpu.make_async_copy(bins.at[rows], held.at[rows], sems.at[4 + i]) for i, rows in enumerate(blocks)]
    for copy in large + small:
        copy.start()
    for copy, rows in zip(large, blocks):
        copy.wait()
        bins_ref[:, rows] = held[rows].astype(F32).astype(BF16).T.astype(F32)
    for copy in small:
        copy.wait()
    stats_of(*columns, stats_ref)
    left_sums_of(lax.axis_index("row"), features, share, bins_ref, stats_ref, out_ref)


def next_kernel(features, share, bins_ref, stats_ref, *refs):
    left_sums_of(lax.axis_index("row"), features, share, bins_ref, stats_ref, refs[-1])


def score_of(grad_t, hess_t, grad_c, hess_c):
    value_t = grad_t / (hess_t + 1.0)
    value_c = grad_c / (hess_c + 1.0)
    spread = value_t - value_c
    return grad_t * value_t + grad_c * value_c + (hess_t + hess_c) * spread * spread


def gain_kernel(kept_ref, came_ref, gain_ref, most_ref, sums_ref, parent_ref):
    share = gain_ref.shape[1]
    x = (kept_ref[...] + came_ref[...]).reshape(share * STATS, BINS)
    source = lax.broadcasted_iota(jnp.int32, (BINS, 2 * BINS), 0)
    target = lax.broadcasted_iota(jnp.int32, (BINS, 2 * BINS), 1)
    carried = (source % LOW == LOW - 1) & ((target >= BINS) | (source // LOW < target // LOW))
    carried = jnp.where(carried, 1.0, 0.0).astype(BF16)
    carry, rest = 0.0, x
    for _ in range(3):
        piece = rest.astype(BF16)
        rest = rest - piece.astype(F32)
        carry = carry + jnp.dot(piece, carried, preferred_element_type=F32)
    sums_ref[...] = (x + carry[:, :BINS]).reshape(sums_ref.shape)
    parent_ref[...] = carry[:, BINS:].reshape(parent_ref.shape)
    tops = []
    for leaf in range(LEAVES):
        left = [sums_ref[:, s * LEAVES + leaf, :] for s in range(4)]
        parent = [parent_ref[:, s * LEAVES + leaf, :] for s in range(4)]
        right = [p - x for p, x in zip(parent, left)]
        gain = score_of(*left) + score_of(*right) - score_of(*parent)
        gain_ref[leaf] = gain
        tops.append(jnp.max(gain, axis=0, keepdims=True))
    top = jnp.max(jnp.concatenate(tops, 0), axis=1, keepdims=True)
    lane = lax.broadcasted_iota(jnp.int32, (LEAVES, BINS), 1)
    leaf = lax.broadcasted_iota(jnp.int32, (LEAVES, BINS), 0)
    line = jnp.sum(jnp.where(lane == leaf, top, 0.0), axis=0, keepdims=True)
    most_ref[...] = jnp.broadcast_to(line, most_ref.shape)


VMEM = pl.BlockSpec(memory_space=pltpu.VMEM)
HBM = pl.BlockSpec(memory_space=pltpu.HBM)
ANY = pl.BlockSpec(memory_space=pl.ANY)
ROOM = pltpu.CompilerParams(vmem_limit_bytes=32 * 2**20)


def body(devices, bin_values, leaf_ids, treated, gradient, hessian):
    rows, feats = bin_values.shape
    ring = lax.axis_size("row")
    bits = ring.bit_length() - 1
    share = feats // ring
    size = feats // 8
    cost = pl.CostEstimate(flops=rows * feats, bytes_accessed=rows * feats // 4, transcendentals=0)

    small = (rows // 128, 128)
    inputs = (bin_values, *(x.reshape(small) for x in (leaf_ids, treated, gradient, hessian)))
    bins, stats, other = pl.pallas_call(
        functools.partial(first_kernel, features_of(bits, share, 1, 3), share),
        out_shape=(
            jax.ShapeDtypeStruct((feats, rows), F32),
            jax.ShapeDtypeStruct((STATS, rows), BF16),
            jax.ShapeDtypeStruct((size, STATS, BINS), F32),
        ),
        in_specs=[HBM] * 5,
        out_specs=(VMEM,) * 3,
        scratch_shapes=[
            pltpu.VMEM(small, jnp.int32),
            pltpu.VMEM(small, jnp.int32),
            pltpu.VMEM(small, BF16),
            pltpu.VMEM(small, BF16),
            pltpu.VMEM((rows, feats), jnp.int32),
            pltpu.SemaphoreType.DMA((4 + BLOCKS,)),
        ],
        compiler_params=ROOM,
        cost_estimate=cost,
        name="stats_and_others",
    )(*(pltpu.with_memory_space_constraint(x, pltpu.HBM) for x in inputs))

    def left_sums(core, nears, *after):
        return pl.pallas_call(
            functools.partial(next_kernel, features_of(bits, share, core, *nears), share),
            out_shape=jax.ShapeDtypeStruct((size * len(nears), STATS, BINS), F32),
            in_specs=[VMEM] * 2 + [ANY] * len(after),
            out_specs=VMEM,
            compiler_params=ROOM,
            cost_estimate=cost,
            name="left_sums_%d_%d" % (core, len(nears) * 10 + nears[0]),
        )(bins, stats, *after)

    def swap(x, mask):
        return lax.ppermute(x, "row", [(i, i ^ mask) for i in range(ring)])

    def halves(x):
        return x[: x.shape[0] // 2], x[x.shape[0] // 2 :]

    came = swap(other, 1)
    diagonal = left_sums(0, [3], other) + came
    other = left_sums(1, [1, 2], diagonal)
    diagonal = swap(diagonal, 2)
    came = halves(swap(other, 1))
    one, two = halves(left_sums(0, [1, 2], other))
    one, two = one + came[0], lax.optimization_barrier(two + diagonal) + came[1]
    other = left_sums(1, [0], one, two)
    one, two = swap(one, 2), swap(two, 4)
    came = swap(other, 1)
    kept = lax.optimization_barrier(left_sums(0, [0], other) + (one + two))
    for stage in range(3, bits):
        (kept, sent), (came, came_sent) = halves(kept), halves(came)
        kept, came = kept + came, swap(sent + came_sent, 1 << stage)

    split_gain, most = pl.pallas_call(
        gain_kernel,
        out_shape=(
            jax.ShapeDtypeStruct((LEAVES, share, BINS), F32),
            jax.ShapeDtypeStruct((devices, BINS), F32),
        ),
        in_specs=[VMEM] * 2,
        out_specs=(VMEM,) * 2,
        scratch_shapes=[pltpu.VMEM((share, STATS, BINS), F32)] * 2,
        compiler_params=ROOM,
        name="gains",
    )(kept, came)
    best = lax.all_to_all(most, ("feat", "row"), 0, 0, tiled=True)
    return split_gain, jnp.max(best, axis=0)[:LEAVES]


def solution(mesh):
    in_specs = (P("row", "feat"), P("row"), P("row"), P("row"), P("row"))
    out_specs = (P(None, ("feat", "row"), None), P())
    return jax.shard_map(
        functools.partial(body, mesh.size), mesh=mesh, in_specs=in_specs, out_specs=out_specs, check_vma=False
    )
```
